128 devices in a mesh: scen: 8 (over x, core), var: 16 (over z, y).
Axes of the slice: x: 4, y: 4, z: 4, core: 2. Of those that a mesh axis runs over, the one named last changes fastest.
Arguments:
- start_point: float32 [1024, 65536], P('scen', 'var'), may hold values from -1 to 1
- multipliers: float32 [1024, 65536], P('scen', 'var'), may hold values from -3 to 3
- cost: bfloat16 [1024, 65536], P('scen', 'var'), may hold values from -6 to 6
- curvature: bfloat16 [1024, 65536], P('scen', 'var'), may hold values from 0.5 to 2
- recourse_rhs: float32 [1024, 512], P('scen'), may hold values from -12 to 12
- technology: bfloat16 [512, 65536], P(None, 'var'), may hold values from -0.0234375 to 0.0234375
- scenario_weight: float32 [1024], P('scen'), may hold values from 1 to 30
- previous_mean: float32 [4, 65536], P(None, 'var'), may hold values from -1 to 1
- active: int32 [1024, 512], P('scen', 'var'), may hold values 0 or 1
Outputs:
- iterate: float32 [1024, 65536], P('scen', 'var')
- new_multipliers: float32 [1024, 65536], P('scen', 'var')
- bundle_mean: float32 [4, 65536], P(None, 'var')
- primal_norm: float32 [], replicated
- dual_norm: float32 [], replicated
The draws below stay inside these ranges and needn't reach their ends.
All inputs are finite; a program needn't handle non-finite values. No bound on the sum of `active` on one device may be relied on, other than what follows from the above.
Results may differ from the reference program's by a relative error of at most 0.0007.
Values sent between devices are 32-bit elements; how exact they have to be, the bound alone decides.
No kernel may reach another device: no remote copies, remote signals or barrier semaphores. Data moves between devices by JAX's collectives and lax.ppermute only.
A program may use at most 64 MiB of HBM per device.

```python
import math
import jax
import jax.numpy as jnp
from jax import lax

V = 65536
M = 512
BLK = 128
G = 4
STEPS = 8
SCENARIOS = 1024


def rising_box(key, count):
    column = jnp.arange(V, dtype=jnp.float32)
    amplitude = (1.0 + 2.0 * column / (V - 1)) / 3.0
    first = jax.random.fold_in(jax.random.fold_in(key, 17), 0)
    values = jax.random.uniform(first, (count, V), jnp.float32, -1.0, 1.0)
    return (values * amplitude[None, :]).astype(jnp.float32)


def draw_start_point(key, part):
    return rising_box(jax.random.fold_in(key, 3), SCENARIOS)


def draw_previous_mean(key, part):
    return rising_box(jax.random.fold_in(key, 5), G)


def draw_scenario_weight(key, part):
    index = jnp.arange(SCENARIOS, dtype=jnp.float32)
    rising = 1.0 + 2.0 * index / (SCENARIOS - 1)
    noise_key = jax.random.fold_in(key, 7)
    base = jnp.exp(jax.random.uniform(noise_key, (SCENARIOS,), jnp.float32, 0.0, 2.302585))
    return jnp.clip(base * rising, 1.0, 30.0).astype(jnp.float32)


def with_ends(drawn, rng, least, high):
    longest = drawn.shape.index(max(drawn.shape))
    spots = []
    for shift in (0, 1):
        where = [jax.random.randint(jax.random.fold_in(rng, axis), (), 0, length) for axis, length in enumerate(drawn.shape)]
        where[longest] = (where[longest] + shift) % drawn.shape[longest]
        spots.append(tuple(where))
    return drawn.at[spots[0]].set(least).at[spots[1]].set(high)


def block_levels(rng, shape, shards, low, top_value):
    def one(position, shards_of):
        draws = jax.random.uniform(jax.random.fold_in(jax.random.fold_in(rng, 6), position), (shards_of,), jnp.float32, low / len(shards), top_value / len(shards))
        return jnp.repeat(jnp.exp(draws), shape[position] // shards_of).reshape((-1,) + (1,) * (len(shape) - position - 1))

    loudness = one(*shards[0])
    for cut in shards[1:]:
        loudness = loudness * one(*cut)
    return loudness


def normal_values(rng, dims, width, reach, shards=(), held_as=jnp.bfloat16):
    array = width * jax.random.normal(rng, dims, jnp.float32)
    if shards:
        array = array * block_levels(rng, dims, shards, -0.22, 0.18)
    return jnp.clip(array, -reach, reach).astype(held_as)


def setup_inputs(seed: int = 0) -> dict:
    key_of = jax.random.split(jax.random.key(seed), 10)
    return {
        "start_point": draw_start_point(jax.random.fold_in(key_of[9], 71), 0),
        "multipliers": normal_values(key_of[1], (SCENARIOS, V), 0.5, 3.0, ((0, 8), (1, 16)), jnp.float32),
        "cost": normal_values(key_of[2], (SCENARIOS, V), 1.0, 6.0, ((0, 8), (1, 16))),
        "curvature": jnp.clip(jnp.exp(math.log(2.0) - 1.3862944 * jax.random.uniform(key_of[3], (SCENARIOS, V), jnp.float32) ** block_levels(key_of[3], (SCENARIOS, V), ((0, 8), (1, 16)), -0.2, 0.2)), 0.5, 2.0).astype(jnp.bfloat16),
        "recourse_rhs": normal_values(key_of[4], (SCENARIOS, M), 3.0, 12.0, ((0, 8),), jnp.float32),
        "technology": normal_values(key_of[5], (M, V), V ** -0.5, 0.0234375, ((1, 16),)),
        "scenario_weight": draw_scenario_weight(jax.random.fold_in(key_of[9], 71), 0),
        "previous_mean": draw_previous_mean(jax.random.fold_in(key_of[9], 71), 0),
        "active": with_ends((jax.random.randint(key_of[8], (SCENARIOS, V // BLK), 0, 4) < 3).astype(jnp.int32), jax.random.fold_in(key_of[8], 1), 0, 1),
    }


highest = lax.Precision.HIGHEST
penalty = 1.0
recourse_scale = 4.0
stride = 0.2
epsilon = 1e-06

def reference(start_point, multipliers, cost, curvature, recourse_rhs, technology, scenario_weight, previous_mean, active):
    node_of = jnp.arange(SCENARIOS, dtype=jnp.int32) // (SCENARIOS // G)
    member = (node_of[:, None] == jnp.arange(G, dtype=jnp.int32)[None, :]).astype(jnp.float32)
    anchor = jnp.dot(member, previous_mean, precision=highest, preferred_element_type=jnp.float32)
    linear = cost.astype(jnp.float32) + multipliers - penalty * anchor
    diagonal = curvature.astype(jnp.float32) + penalty
    active_mask = jnp.repeat(active > 0, BLK, axis=1)
    iterate = start_point
    for sweep in range(STEPS):
        rounded = iterate.astype(jnp.bfloat16)
        image = lax.dot_general(rounded, technology, (((1,), (1,)), ((), ())), preferred_element_type=jnp.float32)
        shortfall = (image - recourse_rhs).astype(jnp.bfloat16)
        pullback = jnp.dot(shortfall, technology, preferred_element_type=jnp.float32)
        stepped = jnp.clip(iterate - stride * (diagonal * iterate + linear + recourse_scale * pullback), -1.0, 1.0)
        iterate = jnp.where(active_mask, stepped, iterate)
    weighted = scenario_weight[:, None] * iterate
    totals = lax.dot_general(member, weighted, (((0,), (0,)), ((), ())), precision=highest, preferred_element_type=jnp.float32)
    bundle_mass = lax.optimization_barrier(jnp.sum(member * scenario_weight[:, None], axis=0))
    bundle_mean = totals / bundle_mass[:, None]
    centred = iterate - jnp.dot(member, bundle_mean, precision=highest, preferred_element_type=jnp.float32)
    spread = jnp.sum(scenario_weight[:, None] * centred * centred)
    drift_sum = jnp.sum(bundle_mass[:, None] * (bundle_mean - previous_mean) ** 2)
    normaliser = jnp.sum(bundle_mass) * V
    primal_norm = jnp.sqrt(spread / normaliser + epsilon)
    dual_norm = penalty * jnp.sqrt(drift_sum / normaliser + epsilon)
    factor = penalty * jnp.sqrt(primal_norm / dual_norm)
    new_multipliers = multipliers + factor * centred
    return (iterate, new_multipliers, bundle_mean, primal_norm, dual_norm)
```

```python
import jax
import jax.numpy as jnp
from jax import lax
from jax.experimental import pallas as pl
from jax.experimental.pallas import tpu as pltpu
from jax.sharding import Mesh
from jax.sharding import PartitionSpec as P

V = 65536
BLK = 128
STEPS = 8
SCEN = ("x", "core")
VAR = ("z", "y")
CHUNK = 512
LANES = 128

penalty = 1.0
recourse_scale = 4.0
stride = 0.2
epsilon = 1e-06

WHOLE = pl.BlockSpec(memory_space=pltpu.VMEM)


def local_call(body, outs, args, flops=0, limit=48 << 20, aliases=None):
    outs = [jax.ShapeDtypeStruct(s, jnp.float32) for s in outs]
    moved = sum(a.size * a.dtype.itemsize for a in args) + sum(4 * o.size for o in outs)
    return pl.pallas_call(
        body,
        out_shape=outs,
        in_specs=[WHOLE] * len(args),
        out_specs=[WHOLE] * len(outs),
        input_output_aliases=aliases or {},
        compiler_params=pltpu.CompilerParams(vmem_limit_bytes=limit),
        cost_estimate=pl.CostEstimate(flops=flops, bytes_accessed=moved, transcendentals=0),
    )(*args)


def image_of(x, tech):
    return lax.dot_general(
        x.astype(jnp.bfloat16), tech, (((1,), (1,)), ((), ())), preferred_element_type=jnp.float32
    )


def first_image(x_ref, tech_ref, image_ref):
    total = None
    for start in range(0, x_ref.shape[1], CHUNK):
        cols = slice(start, start + CHUNK)
        part = image_of(x_ref[:, cols], tech_ref[:, cols])
        total = part if total is None else total + part
    image_ref[...] = total


def coefficients(mult_ref, cost_ref, curv_ref, old_ref, active_ref, scale_ref, shift_ref):
    for block in range(mult_ref.shape[1] // BLK):
        cols = slice(block * BLK, (block + 1) * BLK)
        linear = cost_ref[:, cols].astype(jnp.float32) + mult_ref[:, cols] - penalty * old_ref[:, cols]
        diagonal = curv_ref[:, cols].astype(jnp.float32) + penalty
        on = jnp.broadcast_to(active_ref[:, block : block + 1], linear.shape) > 0
        scale_ref[:, cols] = jnp.where(on, 1.0 - stride * diagonal, 1.0)
        shift_ref[:, cols] = jnp.where(on, -stride * linear, 0.0)


def stepped(start, shortfall, tech, x_ref, scale_ref, shift_ref, gain_ref):
    pullback = jnp.dot(shortfall, tech, preferred_element_type=jnp.float32)
    pieces = []
    for k in range(CHUNK // BLK):
        cols = slice(start + k * BLK, start + (k + 1) * BLK)
        block = (start + k * BLK) // BLK
        gain = jnp.broadcast_to(gain_ref[:, block : block + 1], (x_ref.shape[0], BLK))
        moved = x_ref[:, cols] * scale_ref[:, cols] + shift_ref[:, cols]
        moved = moved - gain * pullback[:, k * BLK : (k + 1) * BLK]
        pieces.append(jnp.clip(moved, -1.0, 1.0))
    return jnp.concatenate(pieces, axis=1)


def step(image_ref, rhs_ref, tech_ref, x_ref, scale_ref, shift_ref, gain_ref, new_ref, out_ref):
    shortfall = (image_ref[...] - rhs_ref[...]).astype(jnp.bfloat16)
    total = None
    for start in range(0, x_ref.shape[1], CHUNK):
        cols = slice(start, start + CHUNK)
        tech = tech_ref[:, cols]
        new = stepped(start, shortfall, tech, x_ref, scale_ref, shift_ref, gain_ref)
        new_ref[:, cols] = new
        part = image_of(new, tech)
        total = part if total is None else total + part
    out_ref[...] = total


def last_step(image_ref, rhs_ref, tech_ref, x_ref, scale_ref, shift_ref, gain_ref, weight_ref, new_ref, row_ref):
    shortfall = (image_ref[...] - rhs_ref[...]).astype(jnp.bfloat16)
    for start in range(0, x_ref.shape[1], CHUNK):
        cols = slice(start, start + CHUNK)
        new = stepped(start, shortfall, tech_ref[:, cols], x_ref, scale_ref, shift_ref, gain_ref)
        new_ref[:, cols] = new
        weight = jnp.broadcast_to(weight_ref[...], (x_ref.shape[0], BLK))
        for k in range(CHUNK // BLK):
            here = slice(start + k * BLK, start + (k + 1) * BLK)
            row_ref[:, here] = jnp.sum(weight * new[:, k * BLK : (k + 1) * BLK], axis=0, keepdims=True)
    mass = jnp.sum(jnp.broadcast_to(weight_ref[...], (x_ref.shape[0], LANES)), axis=0, keepdims=True)
    row_ref[:, x_ref.shape[1] :] = mass


def own_spread(x_ref, row_ref, weight_ref, out_ref):
    width = x_ref.shape[1]
    weight = jnp.broadcast_to(weight_ref[...], (x_ref.shape[0], BLK))
    mass = row_ref[:, width:]
    total = jnp.zeros((x_ref.shape[0], BLK), jnp.float32)
    for start in range(0, width, BLK):
        away = x_ref[:, start : start + BLK] - row_ref[:, start : start + BLK] / mass
        total = total + weight * away * away
    out_ref[...] = jnp.sum(total, axis=0, keepdims=True)


def node_row(own_ref, other_ref, old_ref, spread_ref, leads_ref, out_ref):
    width = old_ref.shape[1]
    own_mass, other_mass = own_ref[:, width:], other_ref[:, width:]
    mass = own_mass + other_mass
    apart = jnp.zeros((1, BLK), jnp.float32)
    drift = jnp.zeros((1, BLK), jnp.float32)
    for start in range(0, width, BLK):
        cols = slice(start, start + BLK)
        own, other = own_ref[:, cols], other_ref[:, cols]
        mean = (own + other) / mass
        out_ref[:, cols] = mean
        gap = own / own_mass - other / other_mass
        apart = apart + gap * gap
        drift = drift + (mean - old_ref[:, cols]) ** 2
    leads = leads_ref[...]
    spread = spread_ref[...] + leads * (own_mass * other_mass / mass) * apart
    drift = leads * mass * drift
    lane = lax.broadcasted_iota(jnp.int32, (1, LANES), 1)
    spread = jnp.sum(spread, axis=1, keepdims=True)
    drift = jnp.sum(drift, axis=1, keepdims=True)
    parts = jnp.where(lane == 0, spread, jnp.where(lane == 1, drift, own_mass))
    out_ref[:, width:] = parts


def new_duals(mult_ref, x_ref, mean_ref, factor_ref, out_ref):
    for start in range(0, x_ref.shape[1], CHUNK):
        cols = slice(start, start + CHUNK)
        factor = factor_ref[:, 0:1]
        out_ref[:, cols] = mult_ref[:, cols] + factor * (x_ref[:, cols] - mean_ref[:, cols])


def to_all(x, axes):
    devices = lax.axis_size(axes)
    return lax.all_to_all(jnp.broadcast_to(x[None], (devices, *x.shape)), axes, 0, 0, tiled=True)


def total_of(partial, axes):
    devices = lax.axis_size(axes)
    rows, width = partial.shape
    pieces = partial.reshape(devices, rows // devices, width)
    arrived = lax.all_to_all(pieces, axes, 0, 0, tiled=True)
    return to_all(jnp.sum(arrived, axis=0), axes).reshape(rows, width)


def shards(
    start_point,
    multipliers,
    cost,
    curvature,
    recourse_rhs,
    technology,
    scenario_weight,
    previous_mean,
    active,
):
    rows, width = start_point.shape
    images = recourse_rhs.shape[1]
    groups = previous_mean.shape[0]
    group_size = lax.axis_size(SCEN) // groups
    position = lax.axis_index(SCEN)
    old_row = lax.dynamic_slice_in_dim(previous_mean, position // group_size, 1, 0)
    weight = scenario_weight[:, None]
    leads = jnp.full((1, LANES), (position % group_size == 0).astype(jnp.float32))
    gain = (stride * recourse_scale) * active.astype(jnp.float32)
    product = 2 * rows * width * images

    (partial,) = local_call(first_image, [(rows, images)], [start_point, technology], product)
    scale, shift = local_call(
        coefficients, [(rows, width)] * 2, [multipliers, cost, curvature, old_row, active], 8 * rows * width
    )
    iterate = start_point
    for sweep in range(STEPS):
        image = total_of(partial, VAR)
        operands = [image, recourse_rhs, technology, iterate, scale, shift, gain]
        if sweep < STEPS - 1:
            iterate, partial = local_call(step, [(rows, width), (rows, images)], operands, 2 * product)
        else:
            iterate, own_row = local_call(
                last_step, [(rows, width), (1, width + LANES)], [*operands, weight], product
            )
    other_row = lax.ppermute(own_row, "core", [(0, 1), (1, 0)])
    (spread,) = local_call(own_spread, [(1, LANES)], [iterate, own_row, weight], 4 * rows * width)
    (row,) = local_call(node_row, [(1, width + LANES)], [own_row, other_row, old_row, spread, leads])
    everyone = to_all(row, SCEN)
    bundle_mean = everyone[::group_size, 0, :width]
    parts = jnp.sum(everyone[:, :, width:], axis=0)
    sums = jnp.sum(to_all(parts, VAR), axis=0)
    normaliser = sums[0, 2] / lax.axis_size(VAR) * V
    primal_norm = jnp.sqrt(sums[0, 0] / normaliser + epsilon)
    dual_norm = penalty * jnp.sqrt(sums[0, 1] / normaliser + epsilon)
    factor = penalty * jnp.sqrt(primal_norm / dual_norm)
    (new_multipliers,) = local_call(
        new_duals,
        [(rows, width)],
        [multipliers, iterate, row[:, :width], jnp.full((1, LANES), factor)],
        3 * rows * width,
    )
    return (iterate, new_multipliers, bundle_mean, primal_norm, dual_norm)


def solution(mesh):
    torus = Mesh(mesh.devices.reshape(4, 2, 4, 4), ("x", "core", "z", "y"))
    return jax.shard_map(
        shards,
        mesh=torus,
        in_specs=(
            P(SCEN, VAR),
            P(SCEN, VAR),
            P(SCEN, VAR),
            P(SCEN, VAR),
            P(SCEN, None),
            P(None, VAR),
            P(SCEN),
            P(None, VAR),
            P(SCEN, VAR),
        ),
        out_specs=(P(SCEN, VAR), P(SCEN, VAR), P(None, VAR), P(), P()),
        check_vma=False,
    )
```

```python
import jax
import jax.numpy as jnp
from jax import lax
from jax.experimental import pallas as pl
from jax.experimental.pallas import tpu as pltpu
from jax.sharding import Mesh
from jax.sharding import PartitionSpec as P

V = 65536
BLK = 128
STEPS = 8
SCEN = ("x", "core")
VAR = ("z", "y")
CHUNK = 512
LANES = 128

penalty = 1.0
recourse_scale = 4.0
stride = 0.2
epsilon = 1e-06

WHOLE = pl.BlockSpec(memory_space=pltpu.VMEM)
FAR = pl.BlockSpec(memory_space=pltpu.HBM)
ROOM = 51 << 20


def local_call(body, outs, args, flops=0, far_in=(), far_out=(), scratch=(), aliases=None):
    outs = [s if isinstance(s, jax.ShapeDtypeStruct) else jax.ShapeDtypeStruct(s, jnp.float32) for s in outs]
    moved = sum(a.size * a.dtype.itemsize for a in args) + sum(o.size * o.dtype.itemsize for o in outs)
    return pl.pallas_call(
        body,
        out_shape=outs,
        in_specs=[FAR if k in far_in else WHOLE for k in range(len(args))],
        out_specs=[FAR if k in far_out else WHOLE for k in range(len(outs))],
        scratch_shapes=list(scratch),
        input_output_aliases=aliases or {},
        compiler_params=pltpu.CompilerParams(vmem_limit_bytes=ROOM),
        cost_estimate=pl.CostEstimate(flops=flops, bytes_accessed=moved, transcendentals=0),
    )(*args)


def landing(array):
    rows, width = array.shape
    chunks = width // CHUNK
    return [pltpu.VMEM((chunks, rows, CHUNK), array.dtype), pltpu.SemaphoreType.DMA((chunks,))]


def cols_of(k):
    return slice(k * CHUNK, (k + 1) * CHUNK)


def fetch(*triples):
    chunks = triples[0][1].shape[0]
    copies = []
    for k in range(chunks):
        row = [
            pltpu.make_async_copy(far.at[pl.ds(0, near.shape[1]), cols_of(k)], near.at[k], sems.at[k])
            for far, near, sems in triples
        ]
        for copy in row:
            copy.start()
        copies.append(row)
    return copies


def image_of(x, tech):
    return lax.dot_general(
        x.astype(jnp.bfloat16), tech, (((1,), (1,)), ((), ())), preferred_element_type=jnp.float32
    )


def first_image(start_far, tech_far, x_ref, image_ref, start_near, start_sem, tech_near, tech_sem):
    copies = fetch((tech_far, tech_near, tech_sem), (start_far, start_near, start_sem))
    total = None
    for k, row in enumerate(copies):
        for copy in row:
            copy.wait()
        x = start_near[k]
        x_ref[:, cols_of(k)] = x
        part = image_of(x, tech_near[k])
        total = part if total is None else total + part
    image_ref[...] = total


def linear_terms(
    mult_far, cost_far, curv_far, old_ref, linear_far, curv_out,
    mult_near, mult_sem, cost_near, cost_sem, curv_near, curv_sem, out_near, out_sem, curv_out_sem,
):
    rows = curv_far.shape[0]
    copies = fetch((mult_far, mult_near, mult_sem), (cost_far, cost_near, cost_sem), (curv_far, curv_near, curv_sem))
    outs = []
    for k, row in enumerate(copies):
        for copy in row:
            copy.wait()
        out_near[k] = cost_near[k].astype(jnp.float32) + mult_near[k] - penalty * old_ref[:, cols_of(k)]
        for near, far, sems in ((out_near, linear_far, out_sem), (curv_near, curv_out, curv_out_sem)):
            out = pltpu.make_async_copy(near.at[k], far.at[pl.ds(0, rows), cols_of(k)], sems.at[k])
            out.start()
            outs.append(out)
    for out in outs:
        out.wait()


def moved(k, shortfall, tech, x_ref, linear, curv, gain_ref):
    pullback = jnp.dot(shortfall, tech, preferred_element_type=jnp.float32)
    x = x_ref[:, cols_of(k)]
    slope = curv.astype(jnp.float32) * x + x + linear + pullback
    pieces = []
    for b in range(CHUNK // BLK):
        block = k * (CHUNK // BLK) + b
        cols = slice(b * BLK, (b + 1) * BLK)
        gain = jnp.broadcast_to(gain_ref[:, block : block + 1], (x_ref.shape[0], BLK))
        pieces.append(jnp.clip(x[:, cols] - gain * slope[:, cols], -1.0, 1.0))
    return jnp.concatenate(pieces, axis=1)


def scaled_shortfall(image_ref, rhs_ref):
    return (image_ref[...] - rhs_ref[...]).astype(jnp.bfloat16) * jnp.bfloat16(recourse_scale)


def step(
    image_ref, rhs_ref, x_ref, gain_ref, tech_far, linear_far, curv_far, new_ref, out_ref,
    tech_near, tech_sem, linear_near, linear_sem, curv_near, curv_sem,
):
    copies = fetch(
        (tech_far, tech_near, tech_sem), (curv_far, curv_near, curv_sem), (linear_far, linear_near, linear_sem)
    )
    shortfall = scaled_shortfall(image_ref, rhs_ref)
    total = None
    for k, row in enumerate(copies):
        for copy in row:
            copy.wait()
        tech = tech_near[k]
        new = moved(k, shortfall, tech, x_ref, linear_near[k], curv_near[k], gain_ref)
        new_ref[:, cols_of(k)] = new
        part = image_of(new, tech)
        total = part if total is None else total + part
    out_ref[...] = total


def last_step(
    image_ref, rhs_ref, x_ref, gain_ref, weight_ref, tech_far, linear_far, curv_far, new_ref, row_ref,
    tech_near, tech_sem, linear_near, linear_sem, curv_near, curv_sem,
):
    copies = fetch(
        (tech_far, tech_near, tech_sem), (curv_far, curv_near, curv_sem), (linear_far, linear_near, linear_sem)
    )
    shortfall = scaled_shortfall(image_ref, rhs_ref)
    rows, width = x_ref.shape
    weight = jnp.broadcast_to(weight_ref[...], (rows, LANES))
    row_ref[:, width:] = jnp.sum(weight, axis=0, keepdims=True)
    for k, row in enumerate(copies):
        for copy in row:
            copy.wait()
        new = moved(k, shortfall, tech_near[k], x_ref, linear_near[k], curv_near[k], gain_ref)
        new_ref[:, cols_of(k)] = new
        for b in range(CHUNK // LANES):
            part = weight * new[:, b * LANES : (b + 1) * LANES]
            start = k * CHUNK + b * LANES
            row_ref[:, start : start + LANES] = jnp.sum(part, axis=0, keepdims=True)


def own_spread(x_ref, row_ref, weight_ref, out_far, out_ref, sem):
    copy = pltpu.make_async_copy(x_ref, out_far, sem)
    copy.start()
    rows, width = x_ref.shape
    weight = jnp.broadcast_to(weight_ref[...], (rows, LANES))
    mass = row_ref[:, width:]
    total = jnp.zeros((rows, LANES), jnp.float32)
    for start in range(0, width, LANES):
        away = x_ref[:, start : start + LANES] - row_ref[:, start : start + LANES] / mass
        total = total + weight * away * away
    out_ref[...] = jnp.sum(total, axis=0, keepdims=True)
    copy.wait()


def node_row(own_ref, other_ref, old_ref, spread_ref, leads_ref, out_ref):
    width = old_ref.shape[1]
    own_mass, other_mass = own_ref[:, width:], other_ref[:, width:]
    mass = own_mass + other_mass
    apart = jnp.zeros((1, LANES), jnp.float32)
    drift = jnp.zeros((1, LANES), jnp.float32)
    for start in range(0, width, LANES):
        cols = slice(start, start + LANES)
        own, other = own_ref[:, cols], other_ref[:, cols]
        mean = (own + other) / mass
        out_ref[:, cols] = mean
        gap = own / own_mass - other / other_mass
        apart = apart + gap * gap
        drift = drift + (mean - old_ref[:, cols]) ** 2
    leads = leads_ref[...]
    spread = spread_ref[...] + leads * (own_mass * other_mass / mass) * apart
    drift = leads * mass * drift
    lane = lax.broadcasted_iota(jnp.int32, (1, LANES), 1)
    spread = jnp.sum(spread, axis=1, keepdims=True)
    drift = jnp.sum(drift, axis=1, keepdims=True)
    out_ref[:, width:] = jnp.where(lane == 0, spread, jnp.where(lane == 1, drift, own_mass))


def new_duals(x_ref, mean_ref, factor_ref, mult_far, out_far, mult_near, mult_sem, out_near, out_sem):
    copies = fetch((mult_far, mult_near, mult_sem))
    factor = factor_ref[:, 0:1]
    outs = []
    for k, row in enumerate(copies):
        for copy in row:
            copy.wait()
        out_near[k] = mult_near[k] + factor * (x_ref[:, cols_of(k)] - mean_ref[:, cols_of(k)])
        out = pltpu.make_async_copy(out_near.at[k], out_far.at[:, cols_of(k)], out_sem.at[k])
        out.start()
        outs.append(out)
    for out in outs:
        out.wait()


def to_all(x, axes):
    devices = lax.axis_size(axes)
    return lax.all_to_all(jnp.broadcast_to(x[None], (devices, *x.shape)), axes, 0, 0, tiled=True)


def total_of(partial, axes):
    devices = lax.axis_size(axes)
    rows, width = partial.shape
    pieces = partial.reshape(devices, rows // devices, width)
    arrived = lax.all_to_all(pieces, axes, 0, 0, tiled=True)
    return to_all(jnp.sum(arrived, axis=0), axes).reshape(rows, width)


def shards(
    start_point,
    multipliers,
    cost,
    curvature,
    recourse_rhs,
    technology,
    scenario_weight,
    previous_mean,
    active,
):
    rows, width = start_point.shape
    images = recourse_rhs.shape[1]
    groups = previous_mean.shape[0]
    group_size = lax.axis_size(SCEN) // groups
    position = lax.axis_index(SCEN)
    old_row = lax.dynamic_slice_in_dim(previous_mean, position // group_size, 1, 0)
    weight = scenario_weight[:, None]
    leads = jnp.full((1, LANES), (position % group_size == 0).astype(jnp.float32))
    gain = stride * active.astype(jnp.float32)
    product = 2 * rows * width * images

    iterate, partial = local_call(
        first_image,
        [(rows, width), (rows, images)],
        [start_point, technology],
        product,
        far_in=(0, 1),
        scratch=landing(start_point) + landing(technology),
    )
    linear, curvature_far = local_call(
        linear_terms,
        [(2 * rows, width), jax.ShapeDtypeStruct((4 * rows, width), curvature.dtype)],
        [multipliers, cost, curvature, old_row],
        2 * rows * width,
        far_in=(0, 1, 2),
        far_out=(0, 1),
        scratch=landing(multipliers) + 2 * landing(cost) + landing(multipliers) + landing(cost)[1:],
    )
    far = [technology, linear, curvature_far]
    near = landing(technology) + landing(multipliers) + landing(curvature)
    for sweep in range(STEPS):
        image = total_of(partial, VAR)
        operands = [image, recourse_rhs, iterate, gain]
        if sweep < STEPS - 1:
            iterate, partial = local_call(
                step,
                [(rows, width), (rows, images)],
                operands + far,
                2 * product,
                far_in=(4, 5, 6),
                scratch=near,
                aliases={2: 0},
            )
        else:
            iterate, own_row = local_call(
                last_step,
                [(rows, width), (1, width + LANES)],
                operands + [weight] + far,
                product,
                far_in=(5, 6, 7),
                scratch=near,
                aliases={2: 0},
            )
    other_row = lax.ppermute(own_row, "core", [(0, 1), (1, 0)])
    final, spread = local_call(
        own_spread,
        [(rows, width), (1, LANES)],
        [iterate, own_row, weight],
        4 * rows * width,
        far_out=(0,),
        scratch=[pltpu.SemaphoreType.DMA],
    )
    (row,) = local_call(node_row, [(1, width + LANES)], [own_row, other_row, old_row, spread, leads])
    everyone = to_all(row, SCEN)
    bundle_mean = everyone[::group_size, 0, :width]
    parts = jnp.sum(everyone[:, :, width:], axis=0)
    sums = jnp.sum(to_all(parts, VAR), axis=0)
    normaliser = sums[0, 2] / lax.axis_size(VAR) * V
    primal_norm = jnp.sqrt(sums[0, 0] / normaliser + epsilon)
    dual_norm = penalty * jnp.sqrt(sums[0, 1] / normaliser + epsilon)
    factor = penalty * jnp.sqrt(primal_norm / dual_norm)
    (new_multipliers,) = local_call(
        new_duals,
        [(rows, width)],
        [iterate, row[:, :width], jnp.full((1, LANES), factor), multipliers],
        3 * rows * width,
        far_in=(3,),
        far_out=(0,),
        scratch=landing(multipliers) + landing(multipliers),
    )
    return (final, new_multipliers, bundle_mean, primal_norm, dual_norm)


def solution(mesh):
    torus = Mesh(mesh.devices.reshape(4, 2, 4, 4), ("x", "core", "z", "y"))
    return jax.shard_map(
        shards,
        mesh=torus,
        in_specs=(
            P(SCEN, VAR),
            P(SCEN, VAR),
            P(SCEN, VAR),
            P(SCEN, VAR),
            P(SCEN, None),
            P(None, VAR),
            P(SCEN),
            P(None, VAR),
            P(SCEN, VAR),
        ),
        out_specs=(P(SCEN, VAR), P(SCEN, VAR), P(None, VAR), P(), P()),
        check_vma=False,
    )
```

```python
import jax
import jax.numpy as jnp
from jax import lax
from jax.experimental import pallas as pl
from jax.experimental.pallas import tpu as pltpu
from jax.sharding import Mesh
from jax.sharding import PartitionSpec as P

V = 65536
STEPS = 8
SCEN = ("x", "core")
VAR = ("z", "y")
LANES = 128
SPANS = ((0, 512), (512, 1024), (1536, 1024), (2560, 1024), (3584, 512))

penalty = 1.0
recourse_scale = 4.0
stride = 0.2
epsilon = 1e-06

WHOLE = pl.BlockSpec(memory_space=pltpu.VMEM)
FAR = pl.BlockSpec(memory_space=pltpu.HBM)
SMALL = pl.BlockSpec(memory_space=pltpu.SMEM)
ROOM = 51 << 20


def local_call(body, outs, args, flops=0, scalar_in=(), far_in=(), far_out=(), scratch=(), aliases=None):
    outs = [s if isinstance(s, jax.ShapeDtypeStruct) else jax.ShapeDtypeStruct(s, jnp.float32) for s in outs]
    moved = sum(a.size * a.dtype.itemsize for a in args) + sum(o.size * o.dtype.itemsize for o in outs)
    return pl.pallas_call(
        body,
        out_shape=outs,
        in_specs=[SMALL if k in scalar_in else FAR if k in far_in else WHOLE for k in range(len(args))],
        out_specs=[FAR if k in far_out else WHOLE for k in range(len(outs))],
        scratch_shapes=list(scratch),
        input_output_aliases=aliases or {},
        compiler_params=pltpu.CompilerParams(vmem_limit_bytes=ROOM),
        cost_estimate=pl.CostEstimate(flops=flops, bytes_accessed=moved, transcendentals=0),
    )(*args)


def landing(array):
    return [pltpu.VMEM(array.shape, array.dtype), pltpu.SemaphoreType.DMA((len(SPANS),))]


def cols_of(k):
    start, size = SPANS[k]
    return slice(start, start + size)


def spans(*triples):
    copies = []
    for k, span in enumerate(SPANS):
        cols = pl.ds(*span)
        row = [
            pltpu.make_async_copy(far.at[pl.ds(0, near.shape[0]), cols], near.at[:, cols], sems.at[k])
            for far, near, sems in triples
        ]
        for copy in row:
            copy.start()
        copies.append(row)
    for k, row in enumerate(copies):
        for copy in row:
            copy.wait()
        yield k, cols_of(k)


def image_of(x, tech):
    return lax.dot_general(
        x.astype(jnp.bfloat16), tech, (((1,), (1,)), ((), ())), preferred_element_type=jnp.float32
    )


def first_image(start_far, tech_far, x_ref, image_ref, start_near, start_sem, tech_near, tech_sem):
    total = None
    for _, cols in spans((tech_far, tech_near, tech_sem), (start_far, start_near, start_sem)):
        x = start_near[:, cols]
        x_ref[:, cols] = x
        part = image_of(x, tech_near[:, cols])
        total = part if total is None else total + part
    image_ref[...] = total


def per_lane_block(cols):
    return [(b, slice(b * LANES, (b + 1) * LANES)) for b in range(cols.start // LANES, cols.stop // LANES)]


def linear_terms(
    mult_far, cost_far, curv_far, old_ref, linear_far, curv_out,
    mult_near, mult_sem, cost_near, cost_sem, curv_near, curv_sem, out_near, out_sem, curv_out_sem,
):
    rows = curv_far.shape[0]
    outs = []
    for k, cols in spans((mult_far, mult_near, mult_sem), (cost_far, cost_near, cost_sem), (curv_far, curv_near, curv_sem)):
        for b, block in per_lane_block(cols):
            anchor = old_ref[b : b + 1, :]
            out_near[:, block] = cost_near[:, block].astype(jnp.float32) + mult_near[:, block] - penalty * anchor
        for near, far, sems in ((out_near, linear_far, out_sem), (curv_near, curv_out, curv_out_sem)):
            out = pltpu.make_async_copy(near.at[:, cols], far.at[pl.ds(0, rows), cols], sems.at[k])
            out.start()
            outs.append(out)
    for out in outs:
        out.wait()


def moved(cols, pullback, x_ref, linear, curv, gain_ref):
    pieces = []
    for b, block in per_lane_block(cols):
        here = slice(block.start - cols.start, block.stop - cols.start)
        x = x_ref[:, block]
        slope = curv[:, block].astype(jnp.float32) * x + x + linear[:, block] + pullback[:, here]
        gain = jnp.broadcast_to(gain_ref[:, b : b + 1], x.shape)
        pieces.append(jnp.clip(x - gain * slope, -1.0, 1.0))
    return jnp.concatenate(pieces, axis=1)


def each_span(arrivals, shortfall, tech_near, finish):
    for k, cols in arrivals:
        finish(k, cols, jnp.dot(shortfall, tech_near[:, cols], preferred_element_type=jnp.float32))


def scaled_shortfall(excess_ref):
    return excess_ref[...].astype(jnp.bfloat16) * jnp.bfloat16(recourse_scale)


def step(
    excess_ref, x_ref, gain_ref, tech_far, linear_far, curv_far, new_ref, out_ref,
    tech_near, tech_sem, linear_near, linear_sem, curv_near, curv_sem,
):
    parts = []

    def finish(k, cols, pullback):
        new = moved(cols, pullback, x_ref, linear_near, curv_near, gain_ref)
        new_ref[:, cols] = new
        part = image_of(new, tech_near[:, cols])
        parts[:] = [parts[0] + part if parts else part]

    each_span(
        spans((tech_far, tech_near, tech_sem), (curv_far, curv_near, curv_sem), (linear_far, linear_near, linear_sem)),
        scaled_shortfall(excess_ref),
        tech_near,
        finish,
    )
    out_ref[...] = parts[0]


def last_step(
    excess_ref, x_ref, gain_ref, weight_ref, tech_far, linear_far, curv_far, new_ref, final_far, row_ref,
    tech_near, tech_sem, linear_near, linear_sem, curv_near, curv_sem, out_sem,
):
    rows, width = x_ref.shape
    blocks = width // LANES
    weight = jnp.broadcast_to(weight_ref[...], (rows, LANES))
    mass = jnp.sum(weight, axis=0, keepdims=True)
    spreads = [jnp.zeros((rows, LANES), jnp.float32)]
    outs = []

    def finish(k, cols, pullback):
        new = moved(cols, pullback, x_ref, linear_near, curv_near, gain_ref)
        new_ref[:, cols] = new
        out = pltpu.make_async_copy(new_ref.at[:, cols], final_far.at[:, cols], out_sem.at[k])
        out.start()
        outs.append(out)
        for b, block in per_lane_block(cols):
            part = new[:, block.start - cols.start : block.stop - cols.start]
            row = jnp.sum(weight * part, axis=0, keepdims=True)
            row_ref[b : b + 1, :] = row
            away = part - row / mass
            spreads[0] = spreads[0] + weight * away * away

    each_span(
        spans((tech_far, tech_near, tech_sem), (curv_far, curv_near, curv_sem), (linear_far, linear_near, linear_sem)),
        scaled_shortfall(excess_ref),
        tech_near,
        finish,
    )
    row_ref[blocks : blocks + 1, :] = mass
    row_ref[blocks + 1 : blocks + 2, :] = jnp.sum(spreads[0], axis=0, keepdims=True)
    for out in outs:
        out.wait()


def node_means(all_ref, old_ref, means_ref, parts_ref):
    groups, blocks, _ = old_ref.shape
    spread, drift, mass = 0.0, 0.0, 0.0
    for g in range(groups):
        first, second = 2 * g, 2 * g + 1
        a, b = all_ref[first, 0:blocks], all_ref[second, 0:blocks]
        mass_a, mass_b = all_ref[first, blocks : blocks + 1], all_ref[second, blocks : blocks + 1]
        both = mass_a + mass_b
        mean = (a + b) / both
        means_ref[g] = mean
        gap = a / mass_a - b / mass_b
        spread = spread + all_ref[first, blocks + 1 : blocks + 2] + all_ref[second, blocks + 1 : blocks + 2]
        spread = spread + (mass_a * mass_b / both) * jnp.sum(gap * gap, axis=0, keepdims=True)
        change = mean - old_ref[g]
        drift = drift + both * jnp.sum(change * change, axis=0, keepdims=True)
        mass = mass + both
    lane = lax.broadcasted_iota(jnp.int32, (1, LANES), 1)
    spread = jnp.sum(spread, axis=1, keepdims=True)
    drift = jnp.sum(drift, axis=1, keepdims=True)
    parts = jnp.where(lane == 0, spread, jnp.where(lane == 1, drift, mass))
    parts_ref[...] = jnp.broadcast_to(parts[None], parts_ref.shape)


def new_duals(
    node_ref, x_ref, means_ref, parts_ref, mult_far, out_far, primal_ref, dual_ref,
    mult_near, mult_sem, out_near, out_sem,
):
    factor = None
    outs = []
    for k, cols in spans((mult_far, mult_near, mult_sem)):
        if factor is None:
            sums = jnp.sum(parts_ref[...], axis=0)[0:1, :]
            normaliser = parts_ref[0, 0:1, 2:3] * V
            primal = jnp.sqrt(sums[:, 0:1] / normaliser + epsilon)
            dual = penalty * jnp.sqrt(sums[:, 1:2] / normaliser + epsilon)
            factor = penalty * jnp.sqrt(primal / dual)
            primal_ref[...] = primal
            dual_ref[...] = dual
            mean = means_ref[node_ref[0]]
        for b, block in per_lane_block(cols):
            out_near[:, block] = mult_near[:, block] + factor * (x_ref[:, block] - mean[b : b + 1, :])
        out = pltpu.make_async_copy(out_near.at[:, cols], out_far.at[:, cols], out_sem.at[k])
        out.start()
        outs.append(out)
    for out in outs:
        out.wait()


def to_all(x, axes):
    devices = lax.axis_size(axes)
    return lax.all_to_all(jnp.broadcast_to(x[None], (devices, *x.shape)), axes, 0, 0, tiled=True)


def excess_of(partial, rhs_rows, axes):
    devices = lax.axis_size(axes)
    rows, width = partial.shape
    pieces = partial.reshape(devices, rows // devices, width)
    arrived = lax.all_to_all(pieces, axes, 0, 0, tiled=True)
    return to_all(jnp.sum(arrived, axis=0) - rhs_rows, axes).reshape(rows, width)


def shards(
    start_point,
    multipliers,
    cost,
    curvature,
    recourse_rhs,
    technology,
    scenario_weight,
    previous_mean,
    active,
):
    rows, width = start_point.shape
    images = recourse_rhs.shape[1]
    groups = previous_mean.shape[0]
    group_size = lax.axis_size(SCEN) // groups
    my_node = lax.axis_index(SCEN) // group_size
    blocks = width // LANES
    old_means = previous_mean.reshape(groups, blocks, LANES)
    old_row = lax.dynamic_index_in_dim(old_means, my_node, 0, keepdims=False)
    owned = rows // lax.axis_size(VAR)
    rhs_rows = lax.dynamic_slice_in_dim(recourse_rhs, lax.axis_index(VAR) * owned, owned, 0)
    rhs_rows = lax.optimization_barrier(rhs_rows)
    weight = scenario_weight[:, None]
    gain = stride * active.astype(jnp.float32)
    product = 2 * rows * width * images
    spread_over = pltpu.SemaphoreType.DMA((len(SPANS),))

    iterate, partial = local_call(
        first_image,
        [(rows, width), (rows, images)],
        [start_point, technology],
        product,
        far_in=(0, 1),
        scratch=landing(start_point) + landing(technology),
    )
    linear, curvature_far = local_call(
        linear_terms,
        [(2 * rows, width), jax.ShapeDtypeStruct((4 * rows, width), curvature.dtype)],
        [multipliers, cost, curvature, old_row],
        2 * rows * width,
        far_in=(0, 1, 2),
        far_out=(0, 1),
        scratch=landing(multipliers) + 2 * landing(cost) + landing(multipliers) + [spread_over],
    )
    far = [technology, linear, curvature_far]
    near = landing(technology) + landing(multipliers) + landing(curvature)
    for sweep in range(STEPS):
        excess = excess_of(partial, rhs_rows, VAR)
        operands = [excess, iterate, gain]
        if sweep < STEPS - 1:
            iterate, partial = local_call(
                step,
                [(rows, width), (rows, images)],
                operands + far,
                2 * product,
                far_in=(3, 4, 5),
                scratch=near,
                aliases={1: 0},
            )
        else:
            iterate, final, own_row = local_call(
                last_step,
                [(rows, width), (rows, width), (blocks + 2, LANES)],
                operands + [weight] + far,
                product,
                far_in=(4, 5, 6),
                far_out=(1,),
                scratch=near + [spread_over],
                aliases={1: 0},
            )
    everyone = to_all(own_row, SCEN)
    means, parts = local_call(
        node_means, [(groups, blocks, LANES), (lax.axis_size(VAR), 8, LANES)], [everyone, old_means]
    )
    bundle_mean = means.reshape(groups, width)
    parts = lax.all_to_all(parts, VAR, 0, 0, tiled=True)
    new_multipliers, primal_norm, dual_norm = local_call(
        new_duals,
        [(rows, width), (1, 1), (1, 1)],
        [jnp.full((1,), my_node, jnp.int32), iterate, means, parts, multipliers],
        3 * rows * width,
        scalar_in=(0,),
        far_in=(4,),
        far_out=(0,),
        scratch=landing(multipliers) + landing(multipliers)[:1] + [spread_over],
    )
    return (final, new_multipliers, bundle_mean, primal_norm[0, 0], dual_norm[0, 0])


def solution(mesh):
    torus = Mesh(mesh.devices.reshape(4, 2, 4, 4), ("x", "core", "z", "y"))
    return jax.shard_map(
        shards,
        mesh=torus,
        in_specs=(
            P(SCEN, VAR),
            P(SCEN, VAR),
            P(SCEN, VAR),
            P(SCEN, VAR),
            P(SCEN, None),
            P(None, VAR),
            P(SCEN),
            P(None, VAR),
            P(SCEN, VAR),
        ),
        out_specs=(P(SCEN, VAR), P(SCEN, VAR), P(None, VAR), P(), P()),
        check_vma=False,
    )
```

```python
import jax
import jax.numpy as jnp
from jax import lax
from jax.experimental import pallas as pl
from jax.experimental.pallas import tpu as pltpu
from jax.sharding import Mesh
from jax.sharding import PartitionSpec as P

V = 65536
STEPS = 8
SCEN = ("x", "core")
VAR = ("z", "y")
LANES = 128
SPANS = ((0, 256), (256, 512), (768, 1024), (1792, 1024), (2816, 768), (3584, 512))

penalty = 1.0
recourse_scale = 4.0
stride = 0.2
epsilon = 1e-06

WHOLE = pl.BlockSpec(memory_space=pltpu.VMEM)
FAR = pl.BlockSpec(memory_space=pltpu.HBM)
SMALL = pl.BlockSpec(memory_space=pltpu.SMEM)
ROOM = 50 << 20


def local_call(body, outs, args, flops=0, scalar_in=(), far_in=(), far_out=(), scratch=(), aliases=None):
    outs = [s if isinstance(s, jax.ShapeDtypeStruct) else jax.ShapeDtypeStruct(s, jnp.float32) for s in outs]
    moved = sum(a.size * a.dtype.itemsize for a in args) + sum(o.size * o.dtype.itemsize for o in outs)
    return pl.pallas_call(
        body,
        out_shape=outs,
        in_specs=[SMALL if k in scalar_in else FAR if k in far_in else WHOLE for k in range(len(args))],
        out_specs=[FAR if k in far_out else WHOLE for k in range(len(outs))],
        scratch_shapes=list(scratch),
        input_output_aliases=aliases or {},
        compiler_params=pltpu.CompilerParams(vmem_limit_bytes=ROOM),
        cost_estimate=pl.CostEstimate(flops=flops, bytes_accessed=moved, transcendentals=0),
    )(*args)


def landing(array):
    return [pltpu.VMEM(array.shape, array.dtype), pltpu.SemaphoreType.DMA((len(SPANS),))]


def cols_of(k):
    start, size = SPANS[k]
    return slice(start, start + size)


def spans(*triples, first=0):
    copies = []
    for k, span in enumerate(SPANS):
        cols = pl.ds(*span)
        row = [
            pltpu.make_async_copy(far.at[pl.ds(0, near.shape[0]), cols], near.at[:, cols], sems.at[k])
            for far, near, sems in triples
            if k >= first
        ]
        for copy in row:
            copy.start()
        copies.append(row)
    for k, row in enumerate(copies):
        for copy in row:
            copy.wait()
        yield k, cols_of(k)


def image_of(x, tech):
    return lax.dot_general(
        x.astype(jnp.bfloat16), tech, (((1,), (1,)), ((), ())), preferred_element_type=jnp.float32
    )


def first_image(start_far, tech_far, x_ref, image_ref, tech_head, start_near, start_sem, tech_near, tech_sem):
    total = None
    for _, cols in spans((tech_far, tech_near, tech_sem), (start_far, start_near, start_sem)):
        x = start_near[:, cols]
        x_ref[:, cols] = x
        part = image_of(x, tech_near[:, cols])
        total = part if total is None else total + part
    image_ref[...] = total
    tech_head[...] = tech_near[:, cols_of(0)]


def per_lane_block(cols):
    return [(b, slice(b * LANES, (b + 1) * LANES)) for b in range(cols.start // LANES, cols.stop // LANES)]


def linear_terms(
    mult_far, cost_far, curv_far, old_ref, linear_far, curv_out, linear_head, curv_head,
    mult_near, mult_sem, cost_near, cost_sem, curv_near, curv_sem, out_near, out_sem, curv_out_sem,
):
    rows = curv_far.shape[0]
    outs = []
    for k, cols in spans((mult_far, mult_near, mult_sem), (cost_far, cost_near, cost_sem), (curv_far, curv_near, curv_sem)):
        for b, block in per_lane_block(cols):
            anchor = old_ref[b : b + 1, :]
            out_near[:, block] = cost_near[:, block].astype(jnp.float32) + mult_near[:, block] - penalty * anchor
        for near, far, sems in ((out_near, linear_far, out_sem), (curv_near, curv_out, curv_out_sem)):
            out = pltpu.make_async_copy(near.at[:, cols], far.at[pl.ds(0, rows), cols], sems.at[k])
            out.start()
            outs.append(out)
    linear_head[...] = out_near[:, cols_of(0)]
    curv_head[...] = curv_near[:, cols_of(0)]
    for out in outs:
        out.wait()


def moved(cols, pullback, x_ref, linear, curv, gain_ref):
    pieces = []
    for b, block in per_lane_block(cols):
        here = slice(block.start - cols.start, block.stop - cols.start)
        x = x_ref[:, block]
        slope = curv[:, block].astype(jnp.float32) * x + x + linear[:, block] + pullback[:, here]
        gain = jnp.broadcast_to(gain_ref[:, b : b + 1], x.shape)
        pieces.append(jnp.clip(x - gain * slope, -1.0, 1.0))
    return jnp.concatenate(pieces, axis=1)


def each_span(arrivals, shortfall, near, heads, finish):
    for k, cols in arrivals:
        tech, linear, curv = near if k else heads
        tech = tech[:, cols]
        finish(k, cols, jnp.dot(shortfall, tech, preferred_element_type=jnp.float32), tech, linear, curv)


def scaled_shortfall(excess_ref):
    return excess_ref[...].astype(jnp.bfloat16) * jnp.bfloat16(recourse_scale)


def step(
    excess_ref, x_ref, gain_ref, tech_head, linear_head, curv_head, tech_far, linear_far, curv_far, new_ref, out_ref,
    tech_near, tech_sem, linear_near, linear_sem, curv_near, curv_sem,
):
    parts = []

    def finish(k, cols, pullback, tech, linear, curv):
        new = moved(cols, pullback, x_ref, linear, curv, gain_ref)
        new_ref[:, cols] = new
        part = image_of(new, tech)
        parts[:] = [parts[0] + part if parts else part]

    each_span(
        spans(
            (tech_far, tech_near, tech_sem), (curv_far, curv_near, curv_sem), (linear_far, linear_near, linear_sem), first=1
        ),
        scaled_shortfall(excess_ref),
        (tech_near, linear_near, curv_near),
        (tech_head, linear_head, curv_head),
        finish,
    )
    out_ref[...] = parts[0]


def last_step(
    excess_ref, x_ref, gain_ref, tech_head, linear_head, curv_head, weight_ref, tech_far, linear_far, curv_far, new_ref, final_far, row_ref,
    tech_near, tech_sem, linear_near, linear_sem, curv_near, curv_sem, out_sem,
):
    rows, width = x_ref.shape
    blocks = width // LANES
    square = (rows, rows)
    diagonal = lax.broadcasted_iota(jnp.int32, square, 0) == lax.broadcasted_iota(jnp.int32, square, 1)
    column = jnp.sum(jnp.where(diagonal, jnp.broadcast_to(weight_ref[...], square), 0.0), axis=1, keepdims=True)
    weight = jnp.broadcast_to(column, (rows, LANES))
    mass = jnp.sum(weight, axis=0, keepdims=True)
    spreads = [jnp.zeros((rows, LANES), jnp.float32)]
    outs = []

    def finish(k, cols, pullback, tech, linear, curv):
        new = moved(cols, pullback, x_ref, linear, curv, gain_ref)
        new_ref[:, cols] = new
        out = pltpu.make_async_copy(new_ref.at[:, cols], final_far.at[:, cols], out_sem.at[k])
        out.start()
        outs.append(out)
        for b, block in per_lane_block(cols):
            part = new[:, block.start - cols.start : block.stop - cols.start]
            row = jnp.sum(weight * part, axis=0, keepdims=True)
            row_ref[b : b + 1, :] = row
            away = part - row / mass
            spreads[0] = spreads[0] + weight * away * away

    each_span(
        spans(
            (tech_far, tech_near, tech_sem), (curv_far, curv_near, curv_sem), (linear_far, linear_near, linear_sem), first=1
        ),
        scaled_shortfall(excess_ref),
        (tech_near, linear_near, curv_near),
        (tech_head, linear_head, curv_head),
        finish,
    )
    row_ref[blocks : blocks + 1, :] = mass
    row_ref[blocks + 1 : blocks + 2, :] = jnp.sum(spreads[0], axis=0, keepdims=True)
    for out in outs:
        out.wait()


def node_means(all_ref, old_ref, means_ref, parts_ref):
    groups, blocks, _ = old_ref.shape
    spread, drift, mass = 0.0, 0.0, 0.0
    for g in range(groups):
        first, second = 2 * g, 2 * g + 1
        a, b = all_ref[first, 0:blocks], all_ref[second, 0:blocks]
        mass_a, mass_b = all_ref[first, blocks : blocks + 1], all_ref[second, blocks : blocks + 1]
        both = mass_a + mass_b
        mean = (a + b) / both
        means_ref[g] = mean
        gap = a / mass_a - b / mass_b
        spread = spread + all_ref[first, blocks + 1 : blocks + 2] + all_ref[second, blocks + 1 : blocks + 2]
        spread = spread + (mass_a * mass_b / both) * jnp.sum(gap * gap, axis=0, keepdims=True)
        change = mean - old_ref[g]
        drift = drift + both * jnp.sum(change * change, axis=0, keepdims=True)
        mass = mass + both
    lane = lax.broadcasted_iota(jnp.int32, (1, LANES), 1)
    spread = jnp.sum(spread, axis=1, keepdims=True)
    drift = jnp.sum(drift, axis=1, keepdims=True)
    parts = jnp.where(lane == 0, spread, jnp.where(lane == 1, drift, mass))
    parts_ref[...] = jnp.broadcast_to(parts[None], parts_ref.shape)


def new_duals(
    node_ref, x_ref, means_ref, parts_ref, mult_far, out_far, primal_ref, dual_ref,
    mult_near, mult_sem, out_near, out_sem,
):
    factor = None
    outs = []
    for k, cols in spans((mult_far, mult_near, mult_sem)):
        if factor is None:
            sums = jnp.sum(parts_ref[...], axis=0)[0:1, :]
            normaliser = parts_ref[0, 0:1, 2:3] * V
            primal = jnp.sqrt(sums[:, 0:1] / normaliser + epsilon)
            dual = penalty * jnp.sqrt(sums[:, 1:2] / normaliser + epsilon)
            factor = penalty * jnp.sqrt(primal / dual)
            primal_ref[...] = primal
            dual_ref[...] = dual
            mean = means_ref[node_ref[0]]
        for b, block in per_lane_block(cols):
            out_near[:, block] = mult_near[:, block] + factor * (x_ref[:, block] - mean[b : b + 1, :])
        out = pltpu.make_async_copy(out_near.at[:, cols], out_far.at[:, cols], out_sem.at[k])
        out.start()
        outs.append(out)
    for out in outs:
        out.wait()


def to_all(x, axes):
    devices = lax.axis_size(axes)
    return lax.all_to_all(jnp.broadcast_to(x[None], (devices, *x.shape)), axes, 0, 0, tiled=True)


def excess_of(partial, rhs_rows, axes):
    devices = lax.axis_size(axes)
    rows, width = partial.shape
    pieces = partial.reshape(devices, rows // devices, width)
    arrived = lax.all_to_all(pieces, axes, 0, 0, tiled=True)
    return to_all(jnp.sum(arrived, axis=0) - rhs_rows, axes).reshape(rows, width)


def shards(
    start_point,
    multipliers,
    cost,
    curvature,
    recourse_rhs,
    technology,
    scenario_weight,
    previous_mean,
    active,
):
    rows, width = start_point.shape
    images = recourse_rhs.shape[1]
    groups = previous_mean.shape[0]
    group_size = lax.axis_size(SCEN) // groups
    my_node = lax.axis_index(SCEN) // group_size
    blocks = width // LANES
    old_means = previous_mean.reshape(groups, blocks, LANES)
    old_row = lax.dynamic_index_in_dim(old_means, my_node, 0, keepdims=False)
    owned = rows // lax.axis_size(VAR)
    rhs_rows = lax.dynamic_slice_in_dim(recourse_rhs, lax.axis_index(VAR) * owned, owned, 0)
    rhs_rows = lax.optimization_barrier(rhs_rows)
    weight = scenario_weight[None, :]
    gain = stride * active.astype(jnp.float32)
    product = 2 * rows * width * images
    spread_over = pltpu.SemaphoreType.DMA((len(SPANS),))

    head = SPANS[0][1]
    iterate, partial, tech_head = local_call(
        first_image,
        [(rows, width), (rows, images), jax.ShapeDtypeStruct((images, head), technology.dtype)],
        [start_point, technology],
        product,
        far_in=(0, 1),
        scratch=landing(start_point) + landing(technology),
    )
    linear, curvature_far, linear_head, curv_head = local_call(
        linear_terms,
        [
            (2 * rows, width),
            jax.ShapeDtypeStruct((4 * rows, width), curvature.dtype),
            (rows, head),
            jax.ShapeDtypeStruct((rows, head), curvature.dtype),
        ],
        [multipliers, cost, curvature, old_row],
        2 * rows * width,
        far_in=(0, 1, 2),
        far_out=(0, 1),
        scratch=landing(multipliers) + 2 * landing(cost) + landing(multipliers) + [spread_over],
    )
    far = [technology, linear, curvature_far]
    near = landing(technology) + landing(multipliers) + landing(curvature)
    for sweep in range(STEPS):
        excess = excess_of(partial, rhs_rows, VAR)
        operands = [excess, iterate, gain, tech_head, linear_head, curv_head]
        if sweep < STEPS - 1:
            iterate, partial = local_call(
                step,
                [(rows, width), (rows, images)],
                operands + far,
                2 * product,
                far_in=(6, 7, 8),
                scratch=near,
                aliases={1: 0},
            )
        else:
            iterate, final, own_row = local_call(
                last_step,
                [(rows, width), (rows, width), (blocks + 2, LANES)],
                operands + [weight] + far,
                product,
                far_in=(7, 8, 9),
                far_out=(1,),
                scratch=near + [spread_over],
                aliases={1: 0},
            )
    everyone = to_all(own_row, SCEN)
    means, parts = local_call(
        node_means, [(groups, blocks, LANES), (lax.axis_size(VAR), 8, LANES)], [everyone, old_means]
    )
    bundle_mean = means.reshape(groups, width)
    parts = lax.all_to_all(parts, VAR, 0, 0, tiled=True)
    new_multipliers, primal_norm, dual_norm = local_call(
        new_duals,
        [(rows, width), (1, 1), (1, 1)],
        [jnp.full((1,), my_node, jnp.int32), iterate, means, parts, multipliers],
        3 * rows * width,
        scalar_in=(0,),
        far_in=(4,),
        far_out=(0,),
        scratch=landing(multipliers) + landing(multipliers)[:1] + [spread_over],
    )
    return (final, new_multipliers, bundle_mean, primal_norm[0, 0], dual_norm[0, 0])


def solution(mesh):
    torus = Mesh(mesh.devices.reshape(4, 2, 4, 4), ("x", "core", "z", "y"))
    return jax.shard_map(
        shards,
        mesh=torus,
        in_specs=(
            P(SCEN, VAR),
            P(SCEN, VAR),
            P(SCEN, VAR),
            P(SCEN, VAR),
            P(SCEN, None),
            P(None, VAR),
            P(SCEN),
            P(None, VAR),
            P(SCEN, VAR),
        ),
        out_specs=(P(SCEN, VAR), P(SCEN, VAR), P(None, VAR), P(), P()),
        check_vma=False,
    )
```

```python
import jax
import jax.numpy as jnp
from jax import lax
from jax.experimental import pallas as pl
from jax.experimental.pallas import tpu as pltpu
from jax.sharding import Mesh
from jax.sharding import PartitionSpec as P

V = 65536
STEPS = 8
SCEN = ("x", "core")
VAR = ("z", "y")
LANES = 128
SPANS = ((0, 256), (256, 512), (768, 1024), (1792, 1024), (2816, 768), (3584, 512))

penalty = 1.0
recourse_scale = 4.0
stride = 0.2
epsilon = 1e-06

WHOLE = pl.BlockSpec(memory_space=pltpu.VMEM)
FAR = pl.BlockSpec(memory_space=pltpu.HBM)
SMALL = pl.BlockSpec(memory_space=pltpu.SMEM)
ROOM = 50 << 20


def local_call(body, outs, args, flops=0, scalar_in=(), far_in=(), far_out=(), scratch=(), aliases=None, room=ROOM):
    outs = [s if isinstance(s, jax.ShapeDtypeStruct) else jax.ShapeDtypeStruct(s, jnp.float32) for s in outs]
    moved = sum(a.size * a.dtype.itemsize for a in args) + sum(o.size * o.dtype.itemsize for o in outs)
    return pl.pallas_call(
        body,
        out_shape=outs,
        in_specs=[SMALL if k in scalar_in else FAR if k in far_in else WHOLE for k in range(len(args))],
        out_specs=[FAR if k in far_out else WHOLE for k in range(len(outs))],
        scratch_shapes=list(scratch),
        input_output_aliases=aliases or {},
        compiler_params=pltpu.CompilerParams(vmem_limit_bytes=room),
        cost_estimate=pl.CostEstimate(flops=flops, bytes_accessed=moved, transcendentals=0),
    )(*args)


def landing(array):
    return [pltpu.VMEM(array.shape, array.dtype), pltpu.SemaphoreType.DMA((len(SPANS),))]


def cols_of(k):
    start, size = SPANS[k]
    return slice(start, start + size)


def spans(*triples, first=0):
    copies = []
    for k, span in enumerate(SPANS):
        cols = pl.ds(*span)
        row = [
            pltpu.make_async_copy(far.at[pl.ds(0, near.shape[0]), cols], near.at[:, cols], sems.at[k])
            for far, near, sems in triples
            if k >= first
        ]
        for copy in row:
            copy.start()
        copies.append(row)
    for k, row in enumerate(copies):
        for copy in row:
            copy.wait()
        yield k, cols_of(k)


def image_of(x, tech):
    return lax.dot_general(
        x.astype(jnp.bfloat16), tech, (((1,), (1,)), ((), ())), preferred_element_type=jnp.float32
    )


def first_image(start_far, tech_far, x_ref, image_ref, tech_head, start_near, start_sem, tech_near, tech_sem):
    total = None
    for _, cols in spans((tech_far, tech_near, tech_sem), (start_far, start_near, start_sem)):
        x = start_near[:, cols]
        x_ref[:, cols] = x
        part = image_of(x, tech_near[:, cols])
        total = part if total is None else total + part
    image_ref[...] = total
    tech_head[...] = tech_near[:, cols_of(0)]


def per_lane_block(cols):
    return [(b, slice(b * LANES, (b + 1) * LANES)) for b in range(cols.start // LANES, cols.stop // LANES)]


def linear_terms(
    mult_far, cost_far, curv_far, old_ref, linear_far, curv_out, linear_head, curv_head,
    mult_near, mult_sem, cost_near, cost_sem, curv_near, curv_sem, out_near, out_sem, curv_out_sem,
):
    rows = curv_far.shape[0]
    outs = []
    for k, cols in spans((mult_far, mult_near, mult_sem), (cost_far, cost_near, cost_sem), (curv_far, curv_near, curv_sem)):
        for b, block in per_lane_block(cols):
            anchor = old_ref[b : b + 1, :]
            out_near[:, block] = cost_near[:, block].astype(jnp.float32) + mult_near[:, block] - penalty * anchor
        for near, far, sems in ((out_near, linear_far, out_sem), (curv_near, curv_out, curv_out_sem)):
            out = pltpu.make_async_copy(near.at[:, cols], far.at[pl.ds(0, rows), cols], sems.at[k])
            out.start()
            outs.append(out)
    linear_head[...] = out_near[:, cols_of(0)]
    curv_head[...] = curv_near[:, cols_of(0)]
    for out in outs:
        out.wait()


def moved(cols, pullback, x_ref, linear, curv, gain_ref):
    pieces = []
    for b, block in per_lane_block(cols):
        here = slice(block.start - cols.start, block.stop - cols.start)
        x = x_ref[:, block]
        slope = curv[:, block].astype(jnp.float32) * x + x + linear[:, block] + pullback[:, here]
        gain = jnp.broadcast_to(gain_ref[:, b : b + 1], x.shape)
        pieces.append(jnp.clip(x - gain * slope, -1.0, 1.0))
    return jnp.concatenate(pieces, axis=1)


def each_span(arrivals, shortfall, near, heads, finish):
    for k, cols in arrivals:
        tech, linear, curv = near if k else heads
        tech = tech[:, cols]
        finish(k, cols, jnp.dot(shortfall, tech, preferred_element_type=jnp.float32), tech, linear, curv)


def scaled_shortfall(excess_ref):
    return excess_ref[...].astype(jnp.bfloat16) * jnp.bfloat16(recourse_scale)


def step(
    excess_ref, x_ref, gain_ref, tech_head, linear_head, curv_head, tech_far, linear_far, curv_far, new_ref, out_ref,
    tech_near, tech_sem, linear_near, linear_sem, curv_near, curv_sem,
):
    parts = []

    def finish(k, cols, pullback, tech, linear, curv):
        new = moved(cols, pullback, x_ref, linear, curv, gain_ref)
        new_ref[:, cols] = new
        part = image_of(new, tech)
        parts[:] = [parts[0] + part if parts else part]

    each_span(
        spans(
            (tech_far, tech_near, tech_sem), (curv_far, curv_near, curv_sem), (linear_far, linear_near, linear_sem), first=1
        ),
        scaled_shortfall(excess_ref),
        (tech_near, linear_near, curv_near),
        (tech_head, linear_head, curv_head),
        finish,
    )
    out_ref[...] = parts[0]


def last_step(
    excess_ref, x_ref, gain_ref, tech_head, linear_head, curv_head, weight_ref, tech_far, linear_far, curv_far, new_ref, final_far, row_ref,
    tech_near, tech_sem, linear_near, linear_sem, curv_near, curv_sem, out_sem,
):
    rows, width = x_ref.shape
    blocks = width // LANES
    square = (rows, rows)
    diagonal = lax.broadcasted_iota(jnp.int32, square, 0) == lax.broadcasted_iota(jnp.int32, square, 1)
    column = jnp.sum(jnp.where(diagonal, jnp.broadcast_to(weight_ref[...], square), 0.0), axis=1, keepdims=True)
    weight = jnp.broadcast_to(column, (rows, LANES))
    mass = jnp.sum(weight, axis=0, keepdims=True)
    spreads = [jnp.zeros((rows, LANES), jnp.float32)]
    outs = []

    def finish(k, cols, pullback, tech, linear, curv):
        new = moved(cols, pullback, x_ref, linear, curv, gain_ref)
        new_ref[:, cols] = new
        out = pltpu.make_async_copy(new_ref.at[:, cols], final_far.at[:, cols], out_sem.at[k])
        out.start()
        outs.append(out)
        for b, block in per_lane_block(cols):
            part = new[:, block.start - cols.start : block.stop - cols.start]
            row = jnp.sum(weight * part, axis=0, keepdims=True)
            row_ref[b : b + 1, :] = row
            away = part - row / mass
            spreads[0] = spreads[0] + weight * away * away

    each_span(
        spans(
            (tech_far, tech_near, tech_sem), (curv_far, curv_near, curv_sem), (linear_far, linear_near, linear_sem), first=1
        ),
        scaled_shortfall(excess_ref),
        (tech_near, linear_near, curv_near),
        (tech_head, linear_head, curv_head),
        finish,
    )
    row_ref[blocks : blocks + 1, :] = mass
    row_ref[blocks + 1 : blocks + 2, :] = jnp.sum(spreads[0], axis=0, keepdims=True)
    for out in outs:
        out.wait()


def node_means(all_ref, old_ref, means_ref, parts_ref):
    groups, blocks, _ = old_ref.shape
    spread, drift, mass = 0.0, 0.0, 0.0
    for g in range(groups):
        first, second = 2 * g, 2 * g + 1
        a, b = all_ref[first, 0:blocks], all_ref[second, 0:blocks]
        mass_a, mass_b = all_ref[first, blocks : blocks + 1], all_ref[second, blocks : blocks + 1]
        both = mass_a + mass_b
        mean = (a + b) / both
        means_ref[g] = mean
        gap = a / mass_a - b / mass_b
        spread = spread + all_ref[first, blocks + 1 : blocks + 2] + all_ref[second, blocks + 1 : blocks + 2]
        spread = spread + (mass_a * mass_b / both) * jnp.sum(gap * gap, axis=0, keepdims=True)
        change = mean - old_ref[g]
        drift = drift + both * jnp.sum(change * change, axis=0, keepdims=True)
        mass = mass + both
    lane = lax.broadcasted_iota(jnp.int32, (1, LANES), 1)
    spread = jnp.sum(spread, axis=1, keepdims=True)
    drift = jnp.sum(drift, axis=1, keepdims=True)
    parts = jnp.where(lane == 0, spread, jnp.where(lane == 1, drift, mass))
    parts_ref[...] = jnp.broadcast_to(parts[None], parts_ref.shape)


def new_duals(
    node_ref, x_ref, means_ref, parts_ref, mult_far, out_far, primal_ref, dual_ref,
    mult_near, mult_sem, out_near, out_sem,
):
    factor = None
    outs = []
    for k, cols in spans((mult_far, mult_near, mult_sem)):
        if factor is None:
            sums = jnp.sum(parts_ref[...], axis=0)[0:1, :]
            normaliser = parts_ref[0, 0:1, 2:3] * V
            primal = jnp.sqrt(sums[:, 0:1] / normaliser + epsilon)
            dual = penalty * jnp.sqrt(sums[:, 1:2] / normaliser + epsilon)
            factor = penalty * jnp.sqrt(primal / dual)
            primal_ref[...] = primal
            dual_ref[...] = dual
            mean = means_ref[node_ref[0]]
        for b, block in per_lane_block(cols):
            out_near[:, block] = mult_near[:, block] + factor * (x_ref[:, block] - mean[b : b + 1, :])
        out = pltpu.make_async_copy(out_near.at[:, cols], out_far.at[:, cols], out_sem.at[k])
        out.start()
        outs.append(out)
    for out in outs:
        out.wait()


def to_all(x, axes):
    devices = lax.axis_size(axes)
    return lax.all_to_all(jnp.broadcast_to(x[None], (devices, *x.shape)), axes, 0, 0, tiled=True)


def excess_of(partial, rhs_rows, axes):
    devices = lax.axis_size(axes)
    rows, width = partial.shape
    pieces = partial.reshape(devices, rows // devices, width)
    arrived = lax.all_to_all(pieces, axes, 0, 0, tiled=True)
    return to_all(jnp.sum(arrived, axis=0) - rhs_rows, axes).reshape(rows, width)


def shards(
    start_point,
    multipliers,
    cost,
    curvature,
    recourse_rhs,
    technology,
    scenario_weight,
    previous_mean,
    active,
):
    rows, width = start_point.shape
    images = recourse_rhs.shape[1]
    groups = previous_mean.shape[0]
    group_size = lax.axis_size(SCEN) // groups
    my_node = lax.axis_index(SCEN) // group_size
    blocks = width // LANES
    old_means = previous_mean.reshape(groups, blocks, LANES)
    old_row = lax.dynamic_index_in_dim(old_means, my_node, 0, keepdims=False)
    owned = rows // lax.axis_size(VAR)
    rhs_rows = lax.dynamic_slice_in_dim(recourse_rhs, lax.axis_index(VAR) * owned, owned, 0)
    rhs_rows = lax.optimization_barrier(rhs_rows)
    weight = scenario_weight[None, :]
    gain = stride * active.astype(jnp.float32)
    product = 2 * rows * width * images
    spread_over = pltpu.SemaphoreType.DMA((len(SPANS),))

    head = SPANS[0][1]
    iterate, partial, tech_head = local_call(
        first_image,
        [(rows, width), (rows, images), jax.ShapeDtypeStruct((images, head), technology.dtype)],
        [start_point, technology],
        product,
        far_in=(0, 1),
        scratch=landing(start_point) + landing(technology),
    )
    linear, curvature_far, linear_head, curv_head = local_call(
        linear_terms,
        [
            (2 * rows, width),
            jax.ShapeDtypeStruct((4 * rows, width), curvature.dtype),
            (rows, head),
            jax.ShapeDtypeStruct((rows, head), curvature.dtype),
        ],
        [multipliers, cost, curvature, old_row],
        2 * rows * width,
        far_in=(0, 1, 2),
        far_out=(0, 1),
        room=52 << 20,
        scratch=landing(multipliers) + 2 * landing(cost) + landing(multipliers) + [spread_over],
    )
    far = [technology, linear, curvature_far]
    near = landing(technology) + landing(multipliers) + landing(curvature)
    for sweep in range(STEPS):
        excess = excess_of(partial, rhs_rows, VAR)
        operands = [excess, iterate, gain, tech_head, linear_head, curv_head]
        if sweep < STEPS - 1:
            iterate, partial = local_call(
                step,
                [(rows, width), (rows, images)],
                operands + far,
                2 * product,
                far_in=(6, 7, 8),
                scratch=near,
                aliases={1: 0},
            )
        else:
            iterate, final, own_row = local_call(
                last_step,
                [(rows, width), (rows, width), (blocks + 2, LANES)],
                operands + [weight] + far,
                product,
                far_in=(7, 8, 9),
                far_out=(1,),
                scratch=near + [spread_over],
                aliases={1: 0},
            )
    everyone = to_all(own_row, SCEN)
    means, parts = local_call(
        node_means, [(groups, blocks, LANES), (lax.axis_size(VAR), 8, LANES)], [everyone, old_means]
    )
    bundle_mean = means.reshape(groups, width)
    parts = lax.all_to_all(parts, VAR, 0, 0, tiled=True)
    new_multipliers, primal_norm, dual_norm = local_call(
        new_duals,
        [(rows, width), (1, 1), (1, 1)],
        [jnp.full((1,), my_node, jnp.int32), iterate, means, parts, multipliers],
        3 * rows * width,
        scalar_in=(0,),
        far_in=(4,),
        far_out=(0,),
        scratch=landing(multipliers) + landing(multipliers)[:1] + [spread_over],
    )
    return (final, new_multipliers, bundle_mean, primal_norm[0, 0], dual_norm[0, 0])


def solution(mesh):
    torus = Mesh(mesh.devices.reshape(4, 2, 4, 4), ("x", "core", "z", "y"))
    return jax.shard_map(
        shards,
        mesh=torus,
        in_specs=(
            P(SCEN, VAR),
            P(SCEN, VAR),
            P(SCEN, VAR),
            P(SCEN, VAR),
            P(SCEN, None),
            P(None, VAR),
            P(SCEN),
            P(None, VAR),
            P(SCEN, VAR),
        ),
        out_specs=(P(SCEN, VAR), P(SCEN, VAR), P(None, VAR), P(), P()),
        check_vma=False,
    )
```

```python
import jax
import jax.numpy as jnp
from jax import lax
from jax.experimental import pallas as pl
from jax.experimental.pallas import tpu as pltpu
from jax.sharding import Mesh
from jax.sharding import PartitionSpec as P

V = 65536
STEPS = 8
SCEN = ("x", "core")
VAR = ("z", "y")
LANES = 128
SPANS = ((0, 256), (256, 512), (768, 1024), (1792, 1024), (2816, 768), (3584, 512))

penalty = 1.0
recourse_scale = 4.0
stride = 0.2
epsilon = 1e-06

WHOLE = pl.BlockSpec(memory_space=pltpu.VMEM)
FAR = pl.BlockSpec(memory_space=pltpu.HBM)
SMALL = pl.BlockSpec(memory_space=pltpu.SMEM)
ROOM = 50 << 20


def local_call(body, outs, args, flops=0, scalar_in=(), far_in=(), far_out=(), scratch=(), aliases=None, room=ROOM):
    outs = [s if isinstance(s, jax.ShapeDtypeStruct) else jax.ShapeDtypeStruct(s, jnp.float32) for s in outs]
    moved = sum(a.size * a.dtype.itemsize for a in args) + sum(o.size * o.dtype.itemsize for o in outs)
    return pl.pallas_call(
        body,
        out_shape=outs,
        in_specs=[SMALL if k in scalar_in else FAR if k in far_in else WHOLE for k in range(len(args))],
        out_specs=[FAR if k in far_out else WHOLE for k in range(len(outs))],
        scratch_shapes=list(scratch),
        input_output_aliases=aliases or {},
        compiler_params=pltpu.CompilerParams(vmem_limit_bytes=room),
        cost_estimate=pl.CostEstimate(flops=flops, bytes_accessed=moved, transcendentals=0),
    )(*args)


def landing(array):
    return [pltpu.VMEM(array.shape, array.dtype), pltpu.SemaphoreType.DMA((len(SPANS),))]


def cols_of(k):
    start, size = SPANS[k]
    return slice(start, start + size)


def spans(*triples, first=0):
    copies = []
    for k, span in enumerate(SPANS):
        cols = pl.ds(*span)
        row = [
            pltpu.make_async_copy(far.at[pl.ds(0, near.shape[0]), cols], near.at[:, cols], sems.at[k])
            for far, near, sems in triples
            if k >= first
        ]
        for copy in row:
            copy.start()
        copies.append(row)

    def arrivals():
        for k, row in enumerate(copies):
            for copy in row:
                copy.wait()
            yield k, cols_of(k)

    return arrivals()


def image_of(x, tech):
    return lax.dot_general(
        x.astype(jnp.bfloat16), tech, (((1,), (1,)), ((), ())), preferred_element_type=jnp.float32
    )


def first_image(start_far, tech_far, x_ref, image_ref, tech_head, start_near, start_sem, tech_near, tech_sem):
    total = None
    for _, cols in spans((tech_far, tech_near, tech_sem), (start_far, start_near, start_sem)):
        x = start_near[:, cols]
        x_ref[:, cols] = x
        part = image_of(x, tech_near[:, cols])
        total = part if total is None else total + part
    image_ref[...] = total
    tech_head[...] = tech_near[:, cols_of(0)]


def per_lane_block(cols):
    return [(b, slice(b * LANES, (b + 1) * LANES)) for b in range(cols.start // LANES, cols.stop // LANES)]


def linear_terms(
    mult_far, cost_far, curv_far, old_ref, linear_far, curv_out, linear_head, curv_head,
    mult_near, mult_sem, cost_near, cost_sem, curv_near, curv_sem, out_near, out_sem, curv_out_sem,
):
    rows = curv_far.shape[0]
    outs = []
    for k, cols in spans((mult_far, mult_near, mult_sem), (cost_far, cost_near, cost_sem), (curv_far, curv_near, curv_sem)):
        for b, block in per_lane_block(cols):
            anchor = old_ref[b : b + 1, :]
            out_near[:, block] = cost_near[:, block].astype(jnp.float32) + mult_near[:, block] - penalty * anchor
        for near, far, sems in ((out_near, linear_far, out_sem), (curv_near, curv_out, curv_out_sem)):
            out = pltpu.make_async_copy(near.at[:, cols], far.at[pl.ds(0, rows), cols], sems.at[k])
            out.start()
            outs.append(out)
    linear_head[...] = out_near[:, cols_of(0)]
    curv_head[...] = curv_near[:, cols_of(0)]
    for out in outs:
        out.wait()


def moved(cols, pullback, x_ref, linear, curv, gain_ref):
    pieces = []
    for b, block in per_lane_block(cols):
        here = slice(block.start - cols.start, block.stop - cols.start)
        x = x_ref[:, block]
        slope = curv[:, block].astype(jnp.float32) * x + x + linear[:, block] + pullback[:, here]
        gain = jnp.broadcast_to(gain_ref[:, b : b + 1], x.shape)
        pieces.append(jnp.clip(x - gain * slope, -1.0, 1.0))
    return jnp.concatenate(pieces, axis=1)


def each_span(arrivals, shortfall, near, heads, finish):
    for k, cols in arrivals:
        tech, linear, curv = near if k else heads
        tech = tech[:, cols]
        finish(k, cols, jnp.dot(shortfall, tech, preferred_element_type=jnp.float32), tech, linear, curv)


def scaled_shortfall(excess_ref):
    return excess_ref[...].astype(jnp.bfloat16) * jnp.bfloat16(recourse_scale)


def step(
    excess_ref, x_ref, gain_ref, tech_head, linear_head, curv_head, tech_far, linear_far, curv_far, new_ref, out_ref,
    tech_near, tech_sem, linear_near, linear_sem, curv_near, curv_sem,
):
    parts = []

    def finish(k, cols, pullback, tech, linear, curv):
        new = moved(cols, pullback, x_ref, linear, curv, gain_ref)
        new_ref[:, cols] = new
        part = image_of(new, tech)
        parts[:] = [parts[0] + part if parts else part]

    each_span(
        spans(
            (tech_far, tech_near, tech_sem), (curv_far, curv_near, curv_sem), (linear_far, linear_near, linear_sem), first=1
        ),
        scaled_shortfall(excess_ref),
        (tech_near, linear_near, curv_near),
        (tech_head, linear_head, curv_head),
        finish,
    )
    out_ref[...] = parts[0]


def last_step(
    excess_ref, x_ref, gain_ref, tech_head, linear_head, curv_head, weight_ref, tech_far, linear_far, curv_far, new_ref, final_far, row_ref,
    tech_near, tech_sem, linear_near, linear_sem, curv_near, curv_sem, out_sem,
):
    rows, width = x_ref.shape
    blocks = width // LANES
    square = (rows, rows)
    diagonal = lax.broadcasted_iota(jnp.int32, square, 0) == lax.broadcasted_iota(jnp.int32, square, 1)
    column = jnp.sum(jnp.where(diagonal, jnp.broadcast_to(weight_ref[...], square), 0.0), axis=1, keepdims=True)
    weight = jnp.broadcast_to(column, (rows, LANES))
    mass = jnp.sum(weight, axis=0, keepdims=True)
    spreads = [jnp.zeros((rows, LANES), jnp.float32)]
    outs = []

    def finish(k, cols, pullback, tech, linear, curv):
        new = moved(cols, pullback, x_ref, linear, curv, gain_ref)
        new_ref[:, cols] = new
        out = pltpu.make_async_copy(new_ref.at[:, cols], final_far.at[:, cols], out_sem.at[k])
        out.start()
        outs.append(out)
        for b, block in per_lane_block(cols):
            part = new[:, block.start - cols.start : block.stop - cols.start]
            row = jnp.sum(weight * part, axis=0, keepdims=True)
            row_ref[b : b + 1, :] = row
            away = part - row / mass
            spreads[0] = spreads[0] + weight * away * away

    each_span(
        spans(
            (tech_far, tech_near, tech_sem), (curv_far, curv_near, curv_sem), (linear_far, linear_near, linear_sem), first=1
        ),
        scaled_shortfall(excess_ref),
        (tech_near, linear_near, curv_near),
        (tech_head, linear_head, curv_head),
        finish,
    )
    row_ref[blocks : blocks + 1, :] = mass
    row_ref[blocks + 1 : blocks + 2, :] = jnp.sum(spreads[0], axis=0, keepdims=True)
    for out in outs:
        out.wait()


def node_means(all_ref, old_ref, means_ref, parts_ref):
    groups, blocks, _ = old_ref.shape
    spread, drift, mass = 0.0, 0.0, 0.0
    for g in range(groups):
        first, second = 2 * g, 2 * g + 1
        a, b = all_ref[first, 0:blocks], all_ref[second, 0:blocks]
        mass_a, mass_b = all_ref[first, blocks : blocks + 1], all_ref[second, blocks : blocks + 1]
        both = mass_a + mass_b
        mean = (a + b) / both
        means_ref[g] = mean
        gap = a / mass_a - b / mass_b
        spread = spread + all_ref[first, blocks + 1 : blocks + 2] + all_ref[second, blocks + 1 : blocks + 2]
        spread = spread + (mass_a * mass_b / both) * jnp.sum(gap * gap, axis=0, keepdims=True)
        change = mean - old_ref[g]
        drift = drift + both * jnp.sum(change * change, axis=0, keepdims=True)
        mass = mass + both
    lane = lax.broadcasted_iota(jnp.int32, (1, LANES), 1)
    spread = jnp.sum(spread, axis=1, keepdims=True)
    drift = jnp.sum(drift, axis=1, keepdims=True)
    parts = jnp.where(lane == 0, spread, jnp.where(lane == 1, drift, mass))
    parts_ref[...] = jnp.broadcast_to(parts[None], parts_ref.shape)


def new_duals(
    node_ref, x_ref, means_ref, parts_ref, mult_far, out_far, primal_ref, dual_ref,
    mult_near, mult_sem, out_near, out_sem,
):
    arrivals = spans((mult_far, mult_near, mult_sem))
    sums = jnp.sum(parts_ref[...], axis=0)[0:1, :]
    normaliser = parts_ref[0, 0:1, 2:3] * V
    primal = jnp.sqrt(sums[:, 0:1] / normaliser + epsilon)
    dual = penalty * jnp.sqrt(sums[:, 1:2] / normaliser + epsilon)
    factor = penalty * jnp.sqrt(primal / dual)
    primal_ref[...] = primal
    dual_ref[...] = dual
    mean = means_ref[node_ref[0]]
    outs = []
    for k, cols in arrivals:
        for b, block in per_lane_block(cols):
            out_near[:, block] = mult_near[:, block] + factor * (x_ref[:, block] - mean[b : b + 1, :])
        out = pltpu.make_async_copy(out_near.at[:, cols], out_far.at[:, cols], out_sem.at[k])
        out.start()
        outs.append(out)
    for out in outs:
        out.wait()


def to_all(x, axes):
    devices = lax.axis_size(axes)
    return lax.all_to_all(jnp.broadcast_to(x[None], (devices, *x.shape)), axes, 0, 0, tiled=True)


def excess_of(partial, rhs_rows, axes):
    devices = lax.axis_size(axes)
    rows, width = partial.shape
    pieces = partial.reshape(devices, rows // devices, width)
    arrived = lax.all_to_all(pieces, axes, 0, 0, tiled=True)
    return to_all(jnp.sum(arrived, axis=0) - rhs_rows, axes).reshape(rows, width)


def shards(
    start_point,
    multipliers,
    cost,
    curvature,
    recourse_rhs,
    technology,
    scenario_weight,
    previous_mean,
    active,
):
    rows, width = start_point.shape
    images = recourse_rhs.shape[1]
    groups = previous_mean.shape[0]
    group_size = lax.axis_size(SCEN) // groups
    my_node = lax.axis_index(SCEN) // group_size
    blocks = width // LANES
    old_means = previous_mean.reshape(groups, blocks, LANES)
    old_row = lax.dynamic_index_in_dim(old_means, my_node, 0, keepdims=False)
    owned = rows // lax.axis_size(VAR)
    rhs_rows = lax.dynamic_slice_in_dim(recourse_rhs, lax.axis_index(VAR) * owned, owned, 0)
    rhs_rows = lax.optimization_barrier(rhs_rows)
    weight = scenario_weight[None, :]
    gain = stride * active.astype(jnp.float32)
    product = 2 * rows * width * images
    spread_over = pltpu.SemaphoreType.DMA((len(SPANS),))

    head = SPANS[0][1]
    iterate, partial, tech_head = local_call(
        first_image,
        [(rows, width), (rows, images), jax.ShapeDtypeStruct((images, head), technology.dtype)],
        [start_point, technology],
        product,
        far_in=(0, 1),
        scratch=landing(start_point) + landing(technology),
    )
    linear, curvature_far, linear_head, curv_head = local_call(
        linear_terms,
        [
            (2 * rows, width),
            jax.ShapeDtypeStruct((4 * rows, width), curvature.dtype),
            (rows, head),
            jax.ShapeDtypeStruct((rows, head), curvature.dtype),
        ],
        [multipliers, cost, curvature, old_row],
        2 * rows * width,
        far_in=(0, 1, 2),
        far_out=(0, 1),
        room=52 << 20,
        scratch=landing(multipliers) + 2 * landing(cost) + landing(multipliers) + [spread_over],
    )
    far = [technology, linear, curvature_far]
    near = landing(technology) + landing(multipliers) + landing(curvature)
    for sweep in range(STEPS):
        excess = excess_of(partial, rhs_rows, VAR)
        operands = [excess, iterate, gain, tech_head, linear_head, curv_head]
        if sweep < STEPS - 1:
            iterate, partial = local_call(
                step,
                [(rows, width), (rows, images)],
                operands + far,
                2 * product,
                far_in=(6, 7, 8),
                scratch=near,
                aliases={1: 0},
            )
        else:
            iterate, final, own_row = local_call(
                last_step,
                [(rows, width), (rows, width), (blocks + 2, LANES)],
                operands + [weight] + far,
                product,
                far_in=(7, 8, 9),
                far_out=(1,),
                scratch=near + [spread_over],
                aliases={1: 0},
            )
    everyone = to_all(own_row, SCEN)
    means, parts = local_call(
        node_means, [(groups, blocks, LANES), (lax.axis_size(VAR), 8, LANES)], [everyone, old_means]
    )
    bundle_mean = means.reshape(groups, width)
    parts = lax.all_to_all(parts, VAR, 0, 0, tiled=True)
    new_multipliers, primal_norm, dual_norm = local_call(
        new_duals,
        [(rows, width), (1, 1), (1, 1)],
        [jnp.full((1,), my_node, jnp.int32), iterate, means, parts, multipliers],
        3 * rows * width,
        scalar_in=(0,),
        far_in=(4,),
        far_out=(0,),
        scratch=landing(multipliers) + landing(multipliers)[:1] + [spread_over],
    )
    return (final, new_multipliers, bundle_mean, primal_norm[0, 0], dual_norm[0, 0])


def solution(mesh):
    torus = Mesh(mesh.devices.reshape(4, 2, 4, 4), ("x", "core", "z", "y"))
    return jax.shard_map(
        shards,
        mesh=torus,
        in_specs=(
            P(SCEN, VAR),
            P(SCEN, VAR),
            P(SCEN, VAR),
            P(SCEN, VAR),
            P(SCEN, None),
            P(None, VAR),
            P(SCEN),
            P(None, VAR),
            P(SCEN, VAR),
        ),
        out_specs=(P(SCEN, VAR), P(SCEN, VAR), P(None, VAR), P(), P()),
        check_vma=False,
    )
```
